256 devices in a mesh: row: 8 (over y_hi, x), col: 32 (over z, y_lo, core).
Axes of the slice: x: 4, y: 4 (y_hi: 2, y_lo: 2; y = y_hi * 2 + y_lo), z: 8, core: 2. Of those that a mesh axis runs over, the one named last changes fastest.
Arguments:
- tokens: bfloat16 [1280, 7168], P('col', 'row'), may hold values from -6 to 6
- cotangent: bfloat16 [1280, 7168], P('col', 'row'), may hold values from -6 to 6
- w_gate: bfloat16 [7168, 16384], P('row', 'col'), may hold values from -0.0625 to 0.0625
- w_up: bfloat16 [7168, 16384], P('row', 'col'), may hold values from -0.0625 to 0.0625
- w_down: bfloat16 [16384, 7168], P('col', 'row'), may hold values from -0.046875 to 0.046875
Outputs:
- grad_tokens: bfloat16 [1280, 7168], P('col', 'row')
- grad_w_gate: bfloat16 [7168, 16384], P('row', 'col')
- grad_w_up: bfloat16 [7168, 16384], P('row', 'col')
- grad_w_down: bfloat16 [16384, 7168], P('col', 'row')
The draws below stay inside these ranges and needn't reach their ends.
All inputs are finite; a program needn't handle non-finite values.
Results may differ from the reference program's by a relative error of at most 0.0049.
Values may be sent and summed in bfloat16 or wider, within the bound.
A program may use at most 64 MiB of HBM per device.

```python
import jax
import jax.numpy as jnp

D = 7168
FF = 16384
TOKENS = 1280


def level_of(rng, extent, pieces, least, largest):
    loudness, own = 1.0, jax.random.fold_in(rng, 6)
    for axis_at, blocks in pieces:
        draws = jnp.exp(jax.random.uniform(jax.random.fold_in(own, axis_at), (blocks,), jnp.float32, least / len(pieces), largest / len(pieces)))
        loudness = loudness * jnp.repeat(draws, extent[axis_at] // blocks).reshape([-1 if axis == axis_at else 1 for axis in range(len(extent))])
    return loudness


def centred(key, dims, deviation, reach, shards=(), kind=jnp.bfloat16):
    entries = deviation * jax.random.normal(key, dims, jnp.float32)
    if shards:
        entries = entries * level_of(key, dims, shards, -0.22, 0.18)
    return jnp.clip(entries, -reach, reach).astype(kind)


def setup_inputs(seed: int = 0) -> dict:
    key_of = jax.random.split(jax.random.key(seed), 6)
    tokens = centred(key_of[0], (TOKENS, D), 1.0, 6.0, ((0, 32), (1, 8)))
    cotangent = centred(key_of[1], (TOKENS, D), 1.0, 6.0, ((0, 32), (1, 8)))
    w_gate = centred(key_of[2], (D, FF), D ** -0.5, 0.0625, ((0, 8), (1, 32)))
    w_up = centred(key_of[3], (D, FF), D ** -0.5, 0.0625, ((0, 8), (1, 32)))
    w_down = centred(key_of[4], (FF, D), FF ** -0.5, 0.046875, ((0, 32), (1, 8)))
    return dict(tokens=tokens, cotangent=cotangent, w_gate=w_gate, w_up=w_up, w_down=w_down)


def reference(tokens, cotangent, w_gate, w_up, w_down):
    gate = jnp.dot(tokens, w_gate, preferred_element_type=jnp.float32)
    up = jnp.dot(tokens, w_up, preferred_element_type=jnp.float32)
    back = jnp.dot(cotangent, w_down.T, preferred_element_type=jnp.float32)
    sigma = jax.nn.sigmoid(gate)
    silu = gate * sigma
    hidden = (silu * up).astype(jnp.bfloat16)
    grad_gate = (back * up * sigma * (1.0 + gate * (1.0 - sigma))).astype(jnp.bfloat16)
    grad_up = (back * silu).astype(jnp.bfloat16)
    grad_w_down = jnp.dot(hidden.T, cotangent, preferred_element_type=jnp.float32).astype(jnp.bfloat16)
    grad_w_gate = jnp.dot(tokens.T, grad_gate, preferred_element_type=jnp.float32).astype(jnp.bfloat16)
    grad_w_up = jnp.dot(tokens.T, grad_up, preferred_element_type=jnp.float32).astype(jnp.bfloat16)
    grad_tokens = jnp.dot(grad_gate, w_gate.T, preferred_element_type=jnp.float32)
    grad_tokens = grad_tokens + jnp.dot(grad_up, w_up.T, preferred_element_type=jnp.float32)
    return grad_tokens.astype(jnp.bfloat16), grad_w_gate, grad_w_up, grad_w_down
```

```python
import jax
import jax.numpy as jnp
from jax import lax
from jax.experimental import pallas as pl
from jax.experimental.pallas import tpu as pltpu
from jax.sharding import PartitionSpec as P

MESH = pl.DeviceIdType.MESH
BF = jnp.bfloat16
F32 = jnp.float32
LL = (((1,), (1,)), ((), ()))
FF = (((0,), (0,)), ((), ()))

SHARD = 40
HALF = 80
PLANE = 160
NZ = 8
NX = 4
ROWS = NZ * PLANE
WIDE = 896
LANE = 128
ORDER = (0, 1, 7, 2, 6, 3, 5, 4)
POS = {s: i for i, s in enumerate(ORDER)}
NSEM = 232


def kernel(
    tok, cot, wg_h, wu_h, wd_h,
    gt_out, gwg_h, gwu_h, gwd_h,
    wg, wu, wd, tc, pf, pb, rb, sy, ry, own, hid,
    dpart, dsend, drecv, zsend, zrecv, zsum, acc, stage, xs, xr, fin, frecv,
    ss, rs, ls,
):
    row, col = lax.axis_index("row"), lax.axis_index("col")
    yh, x = row // NX, row % NX
    z, yl, k = col // 4, (col // 2) % 2, col % 2

    def at(dyh=0, dx=0, dz=0, dyl=0, dk=0):
        r = ((yh + dyh) % 2) * NX + (x + dx + NX) % NX
        c = ((z + dz + NZ) % NZ) * 4 + ((yl + dyl) % 2) * 2 + (k + dk) % 2
        return (r, c)

    def xi(d):
        return (x + d + NX) % NX

    count = [0]
    pending = []

    def send(src, dst, to, hold=True):
        i = count[0]
        count[0] += 1
        copy = pltpu.make_async_remote_copy(
            src_ref=src, dst_ref=dst, send_sem=ss.at[i], recv_sem=rs.at[i], device_id=to, device_id_type=MESH
        )
        copy.start()
        if hold:
            pending.append(copy)
        return copy

    loads = []
    for i, (src, dst) in enumerate(((wg_h, wg), (wu_h, wu), (wd_h, wd))):
        load = pltpu.make_async_copy(src, dst, ls.at[i])
        load.start()
        loads.append(load)

    partners = [at(dx=1), at(dx=-1), at(dyh=1), at(dk=1), at(dyl=1), at(dyl=1, dk=1)]
    partners += [at(dz=d) for d in range(1, NZ)]
    barrier = pltpu.get_barrier_semaphore()
    for p in partners:
        pl.semaphore_signal(barrier, inc=1, device_id=p, device_id_type=MESH)
    pl.semaphore_wait(barrier, len(partners))

    def rows(s, start, size):
        return pl.ds(pl.multiple_of(POS[s] * PLANE + start, 16), size)

    mine = jnp.where(k == 0, tok[...].astype(F32), cot[...].astype(F32))
    xs[...] = jnp.where(k == 0, cot[...].astype(F32), tok[...].astype(F32))
    first = send(xs, xr, at(dk=1))
    first.wait_recv()
    other = xr[...]
    low = jnp.where(k == 0, mine, other)
    high = jnp.where(k == 0, other, mine)
    both = jnp.concatenate([low, high], axis=0).astype(BF)
    tc[k, rows(0, yl * HALF, HALF), :] = both

    halves = (yl * HALF, (1 - yl) * HALF)
    ring = {}
    twin = {}

    def to_twin(s, h):
        ref = tc.at[k, rows(s, halves[h], HALF), :]
        twin[s, h] = send(ref, ref, at(dk=1))

    def to_ring(s, h, step):
        t = (s - step) % NZ
        src = tc.at[k, rows(s, halves[h], HALF), :]
        ring[t, h] = send(src, tc.at[k, rows(t, halves[h], HALF), :], at(dz=step))

    ref0 = tc.at[k, rows(0, halves[0], HALF), :]
    across = send(ref0, ref0, at(dyl=1))
    to_twin(0, 0)
    to_ring(0, 0, -1)
    to_ring(0, 0, 1)
    across.wait_recv()
    to_twin(0, 1)
    to_ring(0, 1, -1)
    to_ring(0, 1, 1)
    for load in loads:
        load.wait()

    def arrive(s):
        for h in (0, 1):
            ring[s, h].wait_recv()
            to_twin(s, h)
            if s in (1, 2) or (s == 3 and h == 0):
                to_ring(s, h, -1)
            if s in (7, 6) or (s == 5 and h == 1):
                to_ring(s, h, 1)

    def ways(s):
        return (1, -1, 1 if POS[s] % 2 == 0 else -1)

    b1, b2, by, cy, cx, cr, gy, dc, dz_ = {}, {}, {}, {}, {}, {}, {}, {}, {}

    def partial(s):
        for h in (0, 1):
            twin[s, h].wait_recv()
        t = tc[0, rows(s, 0, PLANE), :]
        c = tc[1, rows(s, 0, PLANE), :]
        r = rows(s, 0, PLANE)
        for a in range(3):
            if a == 0:
                v = jnp.dot(t, wg[...], preferred_element_type=F32)
            elif a == 1:
                v = jnp.dot(t, wu[...], preferred_element_type=F32)
            else:
                v = lax.dot_general(c, wd[...], LL, preferred_element_type=F32)
            for j in range(NX):
                piece = v[:, j * LANE : (j + 1) * LANE]
                pf[a, j, r, :] = piece
                pb[a, j, r, :] = piece.astype(BF)
            w = ways(s)[a]
            b1[s, a, 0] = send(pb.at[a, xi(2), r, :], rb.at[a, 0, r, :], at(dx=w))
            b1[s, a, 1] = send(pb.at[a, xi(-w), r, :], rb.at[a, 1, r, :], at(dx=-w))

    def relay(s):
        r = rows(s, 0, PLANE)
        for a in range(3):
            w = ways(s)[a]
            b1[s, a, 0].wait_recv()
            pb[a, xi(w), r, :] = (pf[a, xi(w), r, :] + rb[a, 0, r, :].astype(F32)).astype(BF)
            b2[s, a] = send(pb.at[a, xi(w), r, :], rb.at[a, 2, r, :], at(dx=w))

    def cross(s):
        i = POS[s]
        for a in range(3):
            b1[s, a, 1].wait_recv()
            b2[s, a].wait_recv()
            for h in (0, 1):
                r = rows(s, (yh if h == 0 else 1 - yh) * HALF, HALF)
                v = pf[a, x, r, :] + rb[a, 1, r, :].astype(F32) + rb[a, 2, r, :].astype(F32)
                if h == 0:
                    own[i, a] = v
                else:
                    sy[i, a] = v
        by[s] = send(sy.at[i], ry.at[i], at(dyh=1))

    def finish(s):
        i = POS[s]
        by[s].wait_recv()
        gate = own[i, 0] + ry[i, 0]
        up = own[i, 1] + ry[i, 1]
        back = own[i, 2] + ry[i, 2]
        sigma = 1.0 / (1.0 + jnp.exp(-gate))
        silu = gate * sigma
        r = rows(s, yh * HALF, HALF)
        hid[2, x, r, :] = (back * silu).astype(BF)
        w = ways(s)[2]
        src = hid.at[2, x, r, :]
        cx[s, 2, 0] = send(src, src, at(dx=w))
        cx[s, 2, 1] = send(src, src, at(dx=-w))
        hid[0, x, r, :] = (silu * up).astype(BF)
        hid[1, x, r, :] = (back * up * sigma * (1.0 + gate * (1.0 - sigma))).astype(BF)
        src = hid.at[pl.ds(0, 2), x, r, :]
        cy[s] = send(src, src, at(dyh=1))

    def spread(s):
        r = rows(s, 0, PLANE)
        rh = rows(s, yh * HALF, HALF)
        w = ways(s)[2]
        cx[s, 2, 0].wait_recv()
        src = hid.at[2, xi(-w), rh, :]
        cr[s, 2] = send(src, src, at(dx=w))
        cy[s].wait_recv()
        for a in (0, 1):
            w = ways(s)[a]
            src = hid.at[a, x, r, :]
            cx[s, a, 0] = send(src, src, at(dx=w))
            cx[s, a, 1] = send(src, src, at(dx=-w))

    def onward(s):
        r = rows(s, 0, PLANE)
        rh = rows(s, yh * HALF, HALF)
        for a in (0, 1):
            w = ways(s)[a]
            cx[s, a, 0].wait_recv()
            src = hid.at[a, xi(-w), r, :]
            cr[s, a] = send(src, src, at(dx=w))
        cx[s, 2, 1].wait_recv()
        cr[s, 2].wait_recv()
        src = hid.at[2, pl.ds(0, NX), rh, :]
        gy[s] = send(src, src, at(dyh=1))

    def wide(a, r):
        return jnp.concatenate([hid[a, j, r, :] for j in range(NX)], axis=1)

    def down(s):
        i = POS[s]
        r = rows(s, 0, PLANE)
        for a in (0, 1):
            cx[s, a, 1].wait_recv()
            cr[s, a].wait_recv()
        gy[s].wait_recv()
        v = lax.dot_general(wide(1, r), wg[...], LL, preferred_element_type=F32)
        v = v + lax.dot_general(wide(2, r), wu[...], LL, preferred_element_type=F32)
        dpart[i] = v
        dsend[i] = dpart[i, pl.ds(pl.multiple_of((1 - k) * HALF, 8), HALF), :]
        dc[s] = send(dsend.at[i], drecv.at[i], at(dk=1))

    def homeward(s):
        i = POS[s]
        dc[s].wait_recv()
        v = dpart[i, pl.ds(pl.multiple_of(k * HALF, 8), HALF), :] + drecv[i]
        if s == 0:
            zsum[...] = v
        else:
            zsend[i] = v.astype(BF)
            dz_[s] = send(zsend.at[i], zrecv.at[i], at(dz=s))

    def weights(part, last):
        n = ROWS // 2
        r = pl.ds(part * n, n)
        for a, (lhs, out) in enumerate(((None, gwd_h), (1, gwg_h), (2, gwu_h))):
            for j in range(2):
                if a == 0:
                    left = jnp.concatenate([hid[0, 2 * j, r, :], hid[0, 2 * j + 1, r, :]], axis=1)
                    v = lax.dot_general(left, tc[1, r, :], FF, preferred_element_type=F32)
                    place = (pl.ds(j * 256, 256), slice(None))
                    where = acc.at[0, pl.ds(j * 256, 256), :]
                else:
                    right = jnp.concatenate([hid[a, 2 * j, r, :], hid[a, 2 * j + 1, r, :]], axis=1)
                    v = lax.dot_general(right, tc[0, r, :], FF, preferred_element_type=F32)
                    where = acc.at[a, pl.ds(j * 256, 256), :]
                if last:
                    v = where[...] + v
                    if a == 0:
                        stage[0, pl.ds(j * 256, 256), :] = v.astype(BF)
                    else:
                        stage_t = v.T.astype(BF)
                        wstage = wg if a == 1 else wu
                        wstage[:, j * 256 : (j + 1) * 256] = stage_t
                else:
                    where[...] = v
            if last:
                src = stage.at[0] if a == 0 else (wg if a == 1 else wu)
                store = pltpu.make_async_copy(src, out, ls.at[a])
                store.start()
                stores.append(store)

    stores = []
    stages = [arrive, partial, relay, cross, finish, spread, onward, down, homeward]
    n = len(stages)
    for tick in range(NZ + n - 1):
        for j in reversed(range(n)):
            i = tick - j
            if 0 <= i < NZ:
                if not (j == 0 and ORDER[i] == 0):
                    stages[j](ORDER[i])
        if tick == n + 2:
            weights(0, False)
    weights(1, True)

    total = zsum[...]
    for s in ORDER[1:]:
        dz_[s].wait_recv()
        total = total + zrecv[POS[s]].astype(F32)
    fin[...] = total

    def tail(i, src, slot, to):
        return pltpu.make_async_remote_copy(
            src_ref=src, dst_ref=frecv.at[slot], send_sem=ss.at[NSEM + i], recv_sem=rs.at[NSEM + slot],
            device_id=to, device_id_type=MESH,
        )

    lows, highs = fin.at[pl.ds(0, SHARD), :], fin.at[pl.ds(SHARD, SHARD), :]
    home = yl == k
    near = tail(0, fin.at[pl.ds(pl.multiple_of((1 - k) * SHARD, 8), SHARD), :], 0, at(dk=1))
    ycol = z * 4 + (1 - yl) * 2
    far0 = tail(0, lows, 1, (row, ycol))
    far1 = tail(1, highs, 1, (row, ycol + 1))

    @pl.when(home)
    def _():
        near.start()
        far1.wait_recv()
        here = fin[pl.ds(pl.multiple_of(k * SHARD, 8), SHARD), :]
        gt_out[...] = (here + frecv[1]).astype(BF)
        near.wait_send()

    @pl.when(jnp.logical_not(home))
    def _():
        far0.start()
        far1.start()
        near.wait_recv()
        far1.wait_recv()
        gt_out[...] = (frecv[0] + frecv[1]).astype(BF)
        far0.wait_send()
        far1.wait_send()

    for copy in pending:
        copy.wait_send()
    for store in stores:
        store.wait()


def local(tokens, cotangent, w_gate, w_up, w_down):
    vm = pl.BlockSpec(memory_space=pltpu.VMEM)
    hbm = pl.BlockSpec(memory_space=pl.ANY)
    V = pltpu.VMEM
    return pl.pallas_call(
        kernel,
        out_shape=[
            jax.ShapeDtypeStruct((SHARD, WIDE), BF),
            jax.ShapeDtypeStruct((WIDE, 512), BF),
            jax.ShapeDtypeStruct((WIDE, 512), BF),
            jax.ShapeDtypeStruct((512, WIDE), BF),
        ],
        in_specs=[vm, vm, hbm, hbm, hbm],
        out_specs=[vm, hbm, hbm, hbm],
        scratch_shapes=[
            V((WIDE, 512), BF), V((WIDE, 512), BF), V((512, WIDE), BF),
            V((2, ROWS, WIDE), BF),
            V((3, NX, ROWS, LANE), F32),
            V((3, NX, ROWS, LANE), BF),
            V((3, 3, ROWS, LANE), BF),
            V((NZ, 3, HALF, LANE), F32),
            V((NZ, 3, HALF, LANE), F32),
            V((NZ, 3, HALF, LANE), F32),
            V((3, NX, ROWS, LANE), BF),
            V((NZ, PLANE, WIDE), F32),
            V((NZ, HALF, WIDE), F32),
            V((NZ, HALF, WIDE), F32),
            V((NZ, HALF, WIDE), BF),
            V((NZ, HALF, WIDE), BF),
            V((HALF, WIDE), F32),
            V((3, 512, WIDE), F32),
            V((1, 512, WIDE), BF),
            V((SHARD, WIDE), F32), V((SHARD, WIDE), F32),
            V((HALF, WIDE), F32), V((2, SHARD, WIDE), F32),
            pltpu.SemaphoreType.DMA((NSEM + 2,)),
            pltpu.SemaphoreType.DMA((NSEM + 2,)),
            pltpu.SemaphoreType.DMA((3,)),
        ],
        compiler_params=pltpu.CompilerParams(
            collective_id=0, has_side_effects=True, vmem_limit_bytes=62 * 2**20
        ),
        name="ffn_backward",
    )(tokens, cotangent, w_gate, w_up, w_down)


def solution(mesh):
    return jax.shard_map(
        local,
        mesh=mesh,
        in_specs=(P("col", "row"), P("col", "row"), P("row", "col"), P("row", "col"), P("col", "row")),
        out_specs=(P("col", "row"), P("row", "col"), P("row", "col"), P("col", "row")),
        check_vma=False,
    )
```

```python
import jax
import jax.numpy as jnp
from jax import lax
from jax.experimental import pallas as pl
from jax.experimental.pallas import tpu as pltpu
from jax.sharding import PartitionSpec as P

MESH = pl.DeviceIdType.MESH
BF = jnp.bfloat16
F32 = jnp.float32
LL = (((1,), (1,)), ((), ()))
FF = (((0,), (0,)), ((), ()))

SHARD = 40
HALF = 80
PLANE = 160
NZ = 8
NX = 4
ROWS = NZ * PLANE
WIDE = 896
LANE = 128
NSEM = 280
DOWN = (1, 7, 2, 6, 3, 5, 4, 0)
POS = {s: i for i, s in enumerate(DOWN)}
PATHS = {0: (), 1: (2,), 2: (2,), 3: (2,), 4: (2,), 5: (2,), 6: (2,), 7: (2,)}
DIRECT = ()
PROGRAM = (
    ('partial', 0, 0),
    ('start2',),
    ('arrive', 1, 0),
    ('arrive', 7, 0),
    ('partial', 0, 1),
    ('relay', 0, 0),
    ('relay', 0, 1),
    ('arrive', 7, 1),
    ('arrive', 1, 1),
    ('relay', 0, 2),
    ('partial', 7),
    ('partial', 1),
    ('arrive', 2, 0),
    ('arrive', 6, 0),
    ('cross', 0),
    ('relay', 7, 0),
    ('arrive', 6, 1),
    ('arrive', 2, 1),
    ('relay', 7, 1),
    ('relay', 7, 2),
    ('partial', 6),
    ('relay', 1, 0),
    ('partial', 2),
    ('relay', 1, 1),
    ('arrive', 3, 0),
    ('arrive', 5, 0),
    ('relay', 1, 2),
    ('cross', 7),
    ('arrive', 3, 1),
    ('arrive', 5, 1),
    ('relay', 6, 0),
    ('relay', 6, 1),
    ('partial', 3),
    ('relay', 6, 2),
    ('partial', 5),
    ('relay', 2, 1),
    ('arrive', 4, 0),
    ('relay', 2, 0),
    ('relay', 2, 2),
    ('cross', 1),
    ('arrive', 4, 1),
    ('finish', 7),
    ('relay', 3, 0),
    ('partial', 4),
    ('relay', 3, 1),
    ('relay', 3, 2),
    ('cross', 6),
    ('relay', 5, 0),
    ('relay', 5, 1),
    ('finish', 1),
    ('relay', 5, 2),
    ('spreadB', 7),
    ('cross', 2),
    ('finish', 0),
    ('spreadA', 7, 2),
    ('relay', 4, 0),
    ('relay', 4, 1),
    ('relay', 4, 2),
    ('finish', 6),
    ('spreadB', 1),
    ('cross', 3),
    ('cross', 5),
    ('spreadA', 1, 2),
    ('finish', 2),
    ('onward', 7, 0),
    ('onward', 7, 1),
    ('spreadB', 0),
    ('onwardY', 7),
    ('spreadB', 6),
    ('spreadA', 6, 2),
    ('cross', 4),
    ('onward', 1, 0),
    ('finish', 3),
    ('onward', 1, 1),
    ('onwardY', 1),
    ('spreadA', 2, 2),
    ('onward', 0, 0),
    ('finish', 5),
    ('spreadB', 2),
    ('onward', 0, 2),
    ('onward', 0, 1),
    ('onward', 6, 0),
    ('onwardY', 6),
    ('onward', 6, 1),
    ('spreadA', 3, 2),
    ('finish', 4),
    ('onwardY', 2),
    ('spreadA', 5, 2),
    ('spreadB', 3),
    ('onward', 2, 0),
    ('onward', 2, 1),
    ('down', 1),
    ('down', 7),
    ('spreadB', 5),
    ('onwardY', 3),
    ('onwardY', 5),
    ('spreadA', 4, 2),
    ('homeward', 1),
    ('homeward', 7),
    ('onward', 3, 0),
    ('spreadB', 4),
    ('onward', 3, 1),
    ('down', 2),
    ('down', 6),
    ('onward', 5, 0),
    ('onward', 5, 1),
    ('onwardY', 4),
    ('homeward', 2),
    ('homeward', 6),
    ('onward', 4, 0),
    ('onward', 4, 1),
    ('depart', 1),
    ('down', 3),
    ('down', 5),
    ('depart', 7),
    ('homeward', 3),
    ('homeward', 5),
    ('down', 4),
    ('depart', 2),
    ('down', 0),
    ('depart', 6),
    ('homeward', 4),
    ('homeward', 0),
    ('depart', 3),
    ('depart', 5),
    ('weights', 0, 4, True, False),
    ('depart', 4),
    ('depart', 0),
    ('fin',),
    ('weights', 4, 4, False, True),
)


def kernel(
    tok, cot, wg_h, wu_h, wd_h,
    gt_out, gwg_h, gwu_h, gwd_h,
    wg, wu, wd, tc, pf, pb, rb, sy, ry, own, hid,
    dpart, dsend, drecv, zsend, zrecv, zhome, zsum, acc, stage, xs, xr, fin, frecv,
    ss, rs, ls,
):
    row, col = lax.axis_index("row"), lax.axis_index("col")
    yh, x = row // NX, row % NX
    z, yl, k = col // 4, (col // 2) % 2, col % 2

    def at(dyh=0, dx=0, dz=0, dyl=0, dk=0):
        r = ((yh + dyh) % 2) * NX + (x + dx + NX) % NX
        c = ((z + dz + NZ) % NZ) * 4 + ((yl + dyl) % 2) * 2 + (k + dk) % 2
        return (r, c)

    def xi(d):
        return (x + d + NX) % NX

    count = [0]
    pending = []

    def send(src, dst, to, hold=True):
        i = count[0]
        count[0] += 1
        copy = pltpu.make_async_remote_copy(
            src_ref=src, dst_ref=dst, send_sem=ss.at[i], recv_sem=rs.at[i], device_id=to, device_id_type=MESH
        )
        copy.start()
        if hold:
            pending.append(copy)
        return copy

    loads = []
    for i, (src, dst) in enumerate(((wg_h, wg), (wu_h, wu), (wd_h, wd))):
        load = pltpu.make_async_copy(src, dst, ls.at[i])
        load.start()
        loads.append(load)

    partners = [at(dx=1), at(dx=-1), at(dx=2), at(dyh=1), at(dk=1), at(dyl=1)]
    partners += [at(dz=d) for d in range(1, NZ)]
    barrier = pltpu.get_barrier_semaphore()
    for p in partners:
        pl.semaphore_signal(barrier, inc=1, device_id=p, device_id_type=MESH)
    pl.semaphore_wait(barrier, len(partners))

    def rows(s, start, size):
        return pl.ds(pl.multiple_of(POS[s] * PLANE + start, 16), size)

    mine = jnp.where(k == 0, tok[...].astype(F32), cot[...].astype(F32))
    xs[...] = jnp.where(k == 0, cot[...].astype(F32), tok[...].astype(F32))
    first = send(xs, xr, at(dk=1))
    first.wait_recv()
    other = xr[...]
    low = jnp.where(k == 0, mine, other)
    high = jnp.where(k == 0, other, mine)
    both = jnp.concatenate([low, high], axis=0).astype(BF)
    tc[k, rows(0, yl * HALF, HALF), :] = both

    halves = (yl * HALF, (1 - yl) * HALF)
    ring = {}
    twin = {}

    def to_twin(s, h):
        ref = tc.at[k, rows(s, halves[h], HALF), :]
        twin[s, h] = send(ref, ref, at(dk=1))

    def to_ring(s, h, step):
        t = (s - step) % NZ
        src = tc.at[k, rows(s, halves[h], HALF), :]
        ring[t, h] = send(src, tc.at[k, rows(t, halves[h], HALF), :], at(dz=step))

    ref0 = tc.at[k, rows(0, halves[0], HALF), :]
    across = send(ref0, ref0, at(dyl=1))
    to_twin(0, 0)
    to_ring(0, 0, -1)
    to_ring(0, 0, 1)
    def start2():
        across.wait_recv()
        to_twin(0, 1)
        to_ring(0, 1, -1)
        to_ring(0, 1, 1)

    for load in loads:
        load.wait()

    def arrive(s, h):
        ring[s, h].wait_recv()
        to_twin(s, h)
        if s in (1, 2) or (s == 3 and h == 0):
            to_ring(s, h, -1)
        if s in (7, 6) or (s == 5 and h == 1):
            to_ring(s, h, 1)

    def ways(s):
        return (1, -1, 1 if POS[s] % 2 == 0 else -1)

    b1, b2, by, cy, cx, cr, gy, dc, yh_, dz_ = {}, {}, {}, {}, {}, {}, {}, {}, {}, {}
    home = yl == k

    def partial(s, half=None):
        for h in (0, 1) if half is None else (half,):
            twin[s, h].wait_recv()
        r = rows(s, 0, PLANE) if half is None else rows(s, halves[half], HALF)
        t = tc[0, r, :]
        c = tc[1, r, :]
        for a in range(3):
            if a == 0:
                v = jnp.dot(t, wg[...], preferred_element_type=F32)
            elif a == 1:
                v = jnp.dot(t, wu[...], preferred_element_type=F32)
            else:
                v = lax.dot_general(c, wd[...], LL, preferred_element_type=F32)
            for j in range(NX):
                piece = v[:, j * LANE : (j + 1) * LANE]
                pf[a, j, r, :] = piece
                pb[a, j, r, :] = piece.astype(BF)
            w = ways(s)[a]
            if s in DIRECT:
                plan = ((0, w, w), (1, -w, -w), (2, 2, 2))
            else:
                plan = ((0, 2, w), (1, -w, -w))
            for slot, block, to in plan:
                copy = send(pb.at[a, xi(block), r, :], rb.at[a, slot, r, :], at(dx=to))
                b1.setdefault((s, a, slot), []).append(copy)

    def relay(s, a):
        r = rows(s, 0, PLANE)
        w = ways(s)[a]
        for copy in b1[s, a, 0]:
            copy.wait_recv()
        pb[a, xi(w), r, :] = (pf[a, xi(w), r, :] + rb[a, 0, r, :].astype(F32)).astype(BF)
        b2[s, a] = send(pb.at[a, xi(w), r, :], rb.at[a, 2, r, :], at(dx=w))

    def cross(s):
        i = POS[s]
        for a in range(3):
            for slot in (0, 1, 2) if s in DIRECT else (1,):
                for copy in b1[s, a, slot]:
                    copy.wait_recv()
            if s not in DIRECT:
                b2[s, a].wait_recv()
            for h in (0, 1):
                r = rows(s, (yh if h == 0 else 1 - yh) * HALF, HALF)
                v = pf[a, x, r, :] + rb[a, 1, r, :].astype(F32) + rb[a, 2, r, :].astype(F32)
                if s in DIRECT:
                    v = v + rb[a, 0, r, :].astype(F32)
                if h == 0:
                    own[i, a] = v
                else:
                    sy[i, a] = v
        by[s] = send(sy.at[i], ry.at[i], at(dyh=1))

    def finish(s):
        i = POS[s]
        by[s].wait_recv()
        gate = own[i, 0] + ry[i, 0]
        up = own[i, 1] + ry[i, 1]
        back = own[i, 2] + ry[i, 2]
        sigma = 1.0 / (1.0 + jnp.exp(-gate))
        silu = gate * sigma
        r = rows(s, yh * HALF, HALF)
        hid[2, x, r, :] = (back * silu).astype(BF)
        hid[0, x, r, :] = (silu * up).astype(BF)
        hid[1, x, r, :] = (back * up * sigma * (1.0 + gate * (1.0 - sigma))).astype(BF)
        for a in PATHS[s]:
            w = ways(s)[a]
            src = hid.at[a, x, r, :]
            cx[s, a, 0] = send(src, src, at(dx=w))
            cx[s, a, 1] = send(src, src, at(dx=-w))
            if s in DIRECT:
                cr[s, a] = send(src, src, at(dx=2))
        n = 3 - len(PATHS[s])
        if n:
            src = hid.at[pl.ds(0, n), x, r, :]
            cy[s] = send(src, src, at(dyh=1))

    def spreadA(s, a):
        w = ways(s)[a]
        cx[s, a, 0].wait_recv()
        src = hid.at[a, xi(-w), rows(s, yh * HALF, HALF), :]
        cr[s, a] = send(src, src, at(dx=w))

    def spreadB(s):
        r = rows(s, 0, PLANE)
        cy[s].wait_recv()
        for a in range(3 - len(PATHS[s])):
            w = ways(s)[a]
            src = hid.at[a, x, r, :]
            cx[s, a, 0] = send(src, src, at(dx=w))
            cx[s, a, 1] = send(src, src, at(dx=-w))
            if s in DIRECT:
                cr[s, a] = send(src, src, at(dx=2))

    def onward(s, a):
        w = ways(s)[a]
        cx[s, a, 0].wait_recv()
        src = hid.at[a, xi(-w), rows(s, 0, PLANE), :]
        cr[s, a] = send(src, src, at(dx=w))

    def onwardY(s):
        for a in PATHS[s]:
            if s in DIRECT:
                cx[s, a, 0].wait_recv()
            cx[s, a, 1].wait_recv()
            cr[s, a].wait_recv()
        n = len(PATHS[s])
        src = hid.at[pl.ds(3 - n, n), pl.ds(0, NX), rows(s, yh * HALF, HALF), :]
        gy[s] = send(src, src, at(dyh=1))

    def wide(a, r):
        return jnp.concatenate([hid[a, j, r, :] for j in range(NX)], axis=1)

    def down(s):
        i = POS[s]
        r = rows(s, 0, PLANE)
        for a in range(3 - len(PATHS[s])):
            if s in DIRECT:
                cx[s, a, 0].wait_recv()
            cx[s, a, 1].wait_recv()
            cr[s, a].wait_recv()
        if PATHS[s]:
            gy[s].wait_recv()
        v = lax.dot_general(wide(1, r), wg[...], LL, preferred_element_type=F32)
        v = v + lax.dot_general(wide(2, r), wu[...], LL, preferred_element_type=F32)
        dpart[i] = v
        dsend[i] = dpart[i, pl.ds(pl.multiple_of((1 - k) * HALF, 8), HALF), :]
        dc[s] = send(dsend.at[i], drecv.at[i], at(dk=1))

    def homeward(s):
        i = POS[s]
        dc[s].wait_recv()
        v = dpart[i, pl.ds(pl.multiple_of(k * HALF, 8), HALF), :] + drecv[i]
        zsend[i] = v.astype(BF)
        dpart[i, 0:HALF, :] = v
        index = (count[0], count[0] + 1)
        count[0] += 2
        over = pltpu.make_async_remote_copy(
            src_ref=zsend.at[i], dst_ref=zrecv.at[i], send_sem=ss.at[index[0]], recv_sem=rs.at[index[0]],
            device_id=at(dyl=1), device_id_type=MESH,
        )
        yh_[s] = over, index[1]

        @pl.when(jnp.logical_not(home))
        def _():
            over.start()

    def depart(s):
        i = POS[s]
        over, index = yh_[s]
        if s:
            go = pltpu.make_async_remote_copy(
                src_ref=zsend.at[i], dst_ref=zhome.at[i], send_sem=ss.at[index], recv_sem=rs.at[index],
                device_id=at(dz=s), device_id_type=MESH,
            )
            dz_[s] = go

        @pl.when(home)
        def _():
            over.wait_recv()
            v = dpart[i, 0:HALF, :] + zrecv[i].astype(F32)
            if s == 0:
                zsum[...] = v
            else:
                zsend[i] = v.astype(BF)
                go.start()

        @pl.when(jnp.logical_not(home))
        def _():
            over.wait_send()

    def weights(first, count, start, last):
        n = count * PLANE
        r = pl.ds(first * PLANE, n)
        for a, out in enumerate((gwd_h, gwg_h, gwu_h)):
            for j in range(2):
                pair = jnp.concatenate([hid[a, 2 * j, r, :], hid[a, 2 * j + 1, r, :]], axis=1)
                v = lax.dot_general(pair, tc[1 if a == 0 else 0, r, :], FF, preferred_element_type=F32)
                where = acc.at[a, pl.ds(j * 256, 256), :]
                if not start:
                    v = where[...] + v
                if not last:
                    where[...] = v
                elif a == 0:
                    stage[0, pl.ds(j * 256, 256), :] = v.astype(BF)
                else:
                    (wg if a == 1 else wu)[:, j * 256 : (j + 1) * 256] = v.T.astype(BF)
            if last:
                src = stage.at[0] if a == 0 else (wg if a == 1 else wu)
                store = pltpu.make_async_copy(src, out, ls.at[a])
                store.start()
                stores.append(store)

    near = pltpu.make_async_remote_copy(
        src_ref=fin.at[pl.ds(pl.multiple_of((1 - k) * SHARD, 8), SHARD), :], dst_ref=frecv,
        send_sem=ss.at[NSEM], recv_sem=rs.at[NSEM], device_id=at(dk=1), device_id_type=MESH,
    )

    def fin_send():
        @pl.when(home)
        def _():
            total = zsum[...]
            for s in dz_:
                dz_[s].wait_recv()
                total = total + zhome[POS[s]].astype(F32)
            fin[...] = total
            near.start()

    stores = []
    table = dict(
        start2=start2,
        arrive=arrive, partial=partial, relay=relay, cross=cross, finish=finish, spreadA=spreadA, spreadB=spreadB,
        onward=onward, onwardY=onwardY, down=down, homeward=homeward, depart=depart, weights=weights, fin=fin_send,
    )
    for name, *where in PROGRAM:
        table[name](*where)

    @pl.when(home)
    def _():
        gt_out[...] = fin[pl.ds(pl.multiple_of(k * SHARD, 8), SHARD), :].astype(BF)
        near.wait_send()
        for s in dz_:
            dz_[s].wait_send()

    @pl.when(jnp.logical_not(home))
    def _():
        near.wait_recv()
        gt_out[...] = frecv[...].astype(BF)

    for copy in pending:
        copy.wait_send()
    for store in stores:
        store.wait()


def hand_over(g_in, a_in, b_in, c_in, g_out, a_out, b_out, c_out, a, b, c, into, out):
    stays = ((a_in, a, a_out), (b_in, b, b_out), (c_in, c, c_out))
    first = [pltpu.make_async_copy(src, via, into.at[i]) for i, (src, via, _) in enumerate(stays)]
    second = [pltpu.make_async_copy(via, dst, out.at[i]) for i, (_, via, dst) in enumerate(stays)]
    for copy in first:
        copy.start()
    g_out[...] = g_in[...]
    for before, after in zip(first, second):
        before.wait()
        after.start()
    for copy in second:
        copy.wait()


def local(tokens, cotangent, w_gate, w_up, w_down):
    vm = pl.BlockSpec(memory_space=pltpu.VMEM)
    hbm = pl.BlockSpec(memory_space=pl.ANY)
    V = pltpu.VMEM
    shapes = [jax.ShapeDtypeStruct(s, BF) for s in ((SHARD, WIDE), (WIDE, 512), (WIDE, 512), (512, WIDE))]
    grads = pl.pallas_call(
        kernel,
        out_shape=shapes,
        in_specs=[vm, vm, hbm, hbm, hbm],
        out_specs=[vm, hbm, hbm, hbm],
        scratch_shapes=[
            V((WIDE, 512), BF), V((WIDE, 512), BF), V((512, WIDE), BF),
            V((2, ROWS, WIDE), BF),
            V((3, NX, ROWS, LANE), F32),
            V((3, NX, ROWS, LANE), BF),
            V((3, 3, ROWS, LANE), BF),
            V((NZ, 3, HALF, LANE), F32),
            V((NZ, 3, HALF, LANE), F32),
            V((NZ, 3, HALF, LANE), F32),
            V((3, NX, ROWS, LANE), BF),
            V((NZ, PLANE, WIDE), F32),
            V((NZ, HALF, WIDE), F32),
            V((NZ, HALF, WIDE), F32),
            V((NZ, HALF, WIDE), BF),
            V((NZ, HALF, WIDE), BF),
            V((NZ, HALF, WIDE), BF),
            V((HALF, WIDE), F32),
            V((3, 512, WIDE), F32),
            V((1, 512, WIDE), BF),
            V((SHARD, WIDE), F32), V((SHARD, WIDE), F32),
            V((HALF, WIDE), F32), V((SHARD, WIDE), F32),
            pltpu.SemaphoreType.DMA((NSEM + 1,)),
            pltpu.SemaphoreType.DMA((NSEM + 1,)),
            pltpu.SemaphoreType.DMA((3,)),
        ],
        compiler_params=pltpu.CompilerParams(
            collective_id=0, has_side_effects=True, vmem_limit_bytes=62 * 2**20
        ),
        name="ffn_backward",
    )(tokens, cotangent, w_gate, w_up, w_down)
    return pl.pallas_call(
        hand_over,
        out_shape=shapes,
        in_specs=[vm, hbm, hbm, hbm],
        out_specs=[vm, hbm, hbm, hbm],
        scratch_shapes=[V(s.shape, BF) for s in shapes[1:]] + [pltpu.SemaphoreType.DMA((3,))] * 2,
        name="hand_over",
    )(*grads)


def solution(mesh):
    return jax.shard_map(
        local,
        mesh=mesh,
        in_specs=(P("col", "row"), P("col", "row"), P("row", "col"), P("row", "col"), P("col", "row")),
        out_specs=(P("col", "row"), P("row", "col"), P("row", "col"), P("col", "row")),
        check_vma=False,
    )
```

```python
import jax
import jax.numpy as jnp
from jax import lax
from jax.experimental import pallas as pl
from jax.experimental.pallas import tpu as pltpu
from jax.sharding import PartitionSpec as P

MESH = pl.DeviceIdType.MESH
BF = jnp.bfloat16
F32 = jnp.float32
LL = (((1,), (1,)), ((), ()))
FF = (((0,), (0,)), ((), ()))

SHARD = 40
HALF = 80
PLANE = 160
NZ = 8
NX = 4
ROWS = NZ * PLANE
WIDE = 896
LANE = 128
NSEM = 280
DOWN = (1, 7, 2, 6, 3, 5, 4, 0)
POS = {s: i for i, s in enumerate(DOWN)}
PATHS = {0: (), 1: (2,), 2: (2,), 3: (2,), 4: (2,), 5: (2,), 6: (2,), 7: (2,)}
DIRECT = ()
PROGRAM = (
    ('partial', 0, 0),
    ('start2',),
    ('arrive', 7, 0),
    ('arrive', 1, 0),
    ('partial', 0, 1),
    ('arrive', 7, 1),
    ('relay', 0, 2),
    ('arrive', 1, 1),
    ('relay', 0, 0),
    ('partial', 7),
    ('arrive', 6, 0),
    ('partial', 1),
    ('arrive', 6, 1),
    ('arrive', 2, 0),
    ('relay', 0, 1),
    ('partial', 6),
    ('relay', 7, 2),
    ('arrive', 5, 0),
    ('arrive', 2, 1),
    ('relay', 1, 0),
    ('relay', 7, 0),
    ('relay', 1, 1),
    ('relay', 1, 2),
    ('arrive', 5, 1),
    ('arrive', 3, 0),
    ('relay', 6, 0),
    ('cross', 0),
    ('relay', 6, 1),
    ('relay', 7, 1),
    ('partial', 5),
    ('arrive', 3, 1),
    ('cross', 1),
    ('relay', 6, 2),
    ('partial', 3),
    ('cross', 7),
    ('relay', 5, 0),
    ('arrive', 4, 0),
    ('arrive', 4, 1),
    ('relay', 5, 1),
    ('relay', 5, 2),
    ('cross', 6),
    ('partial', 4),
    ('relay', 3, 1),
    ('relay', 3, 2),
    ('relay', 3, 0),
    ('finish', 0),
    ('partial', 2),
    ('finish', 1),
    ('cross', 5),
    ('relay', 4, 2),
    ('relay', 4, 1),
    ('relay', 4, 0),
    ('finish', 6),
    ('cross', 3),
    ('finish', 7),
    ('relay', 2, 0),
    ('relay', 2, 1),
    ('spreadA', 1, 2),
    ('relay', 2, 2),
    ('spreadB', 1),
    ('finish', 5),
    ('cross', 4),
    ('spreadA', 7, 2),
    ('spreadB', 6),
    ('finish', 3),
    ('spreadB', 7),
    ('cross', 2),
    ('spreadA', 6, 2),
    ('onwardY', 7),
    ('spreadB', 5),
    ('spreadA', 3, 2),
    ('spreadA', 5, 2),
    ('onward', 1, 1),
    ('onward', 1, 0),
    ('finish', 4),
    ('onwardY', 6),
    ('spreadB', 3),
    ('finish', 2),
    ('onwardY', 5),
    ('onward', 5, 0),
    ('onward', 5, 1),
    ('onward', 6, 0),
    ('spreadA', 4, 2),
    ('onward', 3, 0),
    ('onwardY', 3),
    ('spreadB', 4),
    ('spreadA', 2, 2),
    ('onward', 3, 1),
    ('onwardY', 1),
    ('onwardY', 4),
    ('spreadB', 2),
    ('onward', 7, 1),
    ('down', 5),
    ('onward', 4, 0),
    ('onward', 4, 1),
    ('onwardY', 2),
    ('onward', 6, 1),
    ('onward', 7, 0),
    ('spreadB', 0),
    ('down', 3),
    ('homeward', 5),
    ('down', 1),
    ('homeward', 3),
    ('onward', 2, 1),
    ('onward', 2, 0),
    ('down', 4),
    ('homeward', 1),
    ('down', 7),
    ('depart', 5),
    ('down', 6),
    ('homeward', 4),
    ('depart', 3),
    ('onward', 0, 2),
    ('down', 2),
    ('homeward', 6),
    ('homeward', 2),
    ('depart', 4),
    ('onward', 0, 0),
    ('onward', 0, 1),
    ('weights', 0, 4, True, False, 0),
    ('homeward', 7),
    ('depart', 6),
    ('weights', 0, 4, True, False, 1),
    ('depart', 2),
    ('down', 0),
    ('depart', 7),
    ('weights', 0, 4, True, False, 2),
    ('weights', 4, 4, False, True, 0),
    ('homeward', 0),
    ('depart', 1),
    ('weights', 4, 4, False, True, 1),
    ('weights', 4, 4, False, True, 2),
    ('depart', 0),
    ('fin',),
)


def kernel(
    tok, cot, wg_h, wu_h, wd_h,
    gt_out, gwg_h, gwu_h, gwd_h,
    wg, wu, wd, tc, pf, pb, rb, sy, ry, own, hid,
    dpart, dsend, drecv, zsend, zrecv, zhome, zsum, acc, stage, xs, xr, fin, frecv,
    ss, rs, ls,
):
    row, col = lax.axis_index("row"), lax.axis_index("col")
    yh, x = row // NX, row % NX
    z, yl, k = col // 4, (col // 2) % 2, col % 2

    def at(dyh=0, dx=0, dz=0, dyl=0, dk=0):
        r = ((yh + dyh) % 2) * NX + (x + dx + NX) % NX
        c = ((z + dz + NZ) % NZ) * 4 + ((yl + dyl) % 2) * 2 + (k + dk) % 2
        return (r, c)

    def xi(d):
        return (x + d + NX) % NX

    count = [0]
    pending = []

    def send(src, dst, to, hold=True):
        i = count[0]
        count[0] += 1
        copy = pltpu.make_async_remote_copy(
            src_ref=src, dst_ref=dst, send_sem=ss.at[i], recv_sem=rs.at[i], device_id=to, device_id_type=MESH
        )
        copy.start()
        if hold:
            pending.append(copy)
        return copy

    loads = []
    for i, (src, dst) in enumerate(((wg_h, wg), (wu_h, wu), (wd_h, wd))):
        load = pltpu.make_async_copy(src, dst, ls.at[i])
        load.start()
        loads.append(load)

    partners = [at(dx=1), at(dx=-1), at(dx=2), at(dyh=1), at(dk=1), at(dyl=1)]
    partners += [at(dz=d) for d in range(1, NZ)]
    barrier = pltpu.get_barrier_semaphore()
    for p in partners:
        pl.semaphore_signal(barrier, inc=1, device_id=p, device_id_type=MESH)
    pl.semaphore_wait(barrier, len(partners))

    def rows(s, start, size):
        return pl.ds(pl.multiple_of(POS[s] * PLANE + start, 16), size)

    mine = jnp.where(k == 0, tok[...].astype(F32), cot[...].astype(F32))
    xs[...] = jnp.where(k == 0, cot[...].astype(F32), tok[...].astype(F32))
    first = send(xs, xr, at(dk=1))
    first.wait_recv()
    other = xr[...]
    low = jnp.where(k == 0, mine, other)
    high = jnp.where(k == 0, other, mine)
    both = jnp.concatenate([low, high], axis=0).astype(BF)
    tc[k, rows(0, yl * HALF, HALF), :] = both

    halves = (yl * HALF, (1 - yl) * HALF)
    ring = {}
    twin = {}

    def to_twin(s, h):
        ref = tc.at[k, rows(s, halves[h], HALF), :]
        twin[s, h] = send(ref, ref, at(dk=1))

    def to_ring(s, h, step):
        t = (s - step) % NZ
        src = tc.at[k, rows(s, halves[h], HALF), :]
        ring[t, h] = send(src, tc.at[k, rows(t, halves[h], HALF), :], at(dz=step))

    ref0 = tc.at[k, rows(0, halves[0], HALF), :]
    across = send(ref0, ref0, at(dyl=1))
    to_twin(0, 0)
    to_ring(0, 0, -1)
    to_ring(0, 0, 1)
    def start2():
        across.wait_recv()
        to_twin(0, 1)
        to_ring(0, 1, -1)
        to_ring(0, 1, 1)

    for load in loads:
        load.wait()

    def arrive(s, h):
        ring[s, h].wait_recv()
        to_twin(s, h)
        if s in (1, 2) or (s == 3 and h == 0):
            to_ring(s, h, -1)
        if s in (7, 6) or (s == 5 and h == 1):
            to_ring(s, h, 1)

    def ways(s):
        return (1, -1, 1 if POS[s] % 2 == 0 else -1)

    b1, b2, by, cy, cx, cr, gy, dc, yh_, dz_ = {}, {}, {}, {}, {}, {}, {}, {}, {}, {}
    home = yl == k

    def partial(s, half=None):
        for h in (0, 1) if half is None else (half,):
            twin[s, h].wait_recv()
        r = rows(s, 0, PLANE) if half is None else rows(s, halves[half], HALF)
        t = tc[0, r, :]
        c = tc[1, r, :]
        for a in range(3):
            if a == 0:
                v = jnp.dot(t, wg[...], preferred_element_type=F32)
            elif a == 1:
                v = jnp.dot(t, wu[...], preferred_element_type=F32)
            else:
                v = lax.dot_general(c, wd[...], LL, preferred_element_type=F32)
            for j in range(NX):
                piece = v[:, j * LANE : (j + 1) * LANE]
                pf[a, j, r, :] = piece
                pb[a, j, r, :] = piece.astype(BF)
            w = ways(s)[a]
            if s in DIRECT:
                plan = ((0, w, w), (1, -w, -w), (2, 2, 2))
            else:
                plan = ((0, 2, w), (1, -w, -w))
            for slot, block, to in plan:
                copy = send(pb.at[a, xi(block), r, :], rb.at[a, slot, r, :], at(dx=to))
                b1.setdefault((s, a, slot), []).append(copy)

    def relay(s, a):
        r = rows(s, 0, PLANE)
        w = ways(s)[a]
        for copy in b1[s, a, 0]:
            copy.wait_recv()
        pb[a, xi(w), r, :] = (pf[a, xi(w), r, :] + rb[a, 0, r, :].astype(F32)).astype(BF)
        b2[s, a] = send(pb.at[a, xi(w), r, :], rb.at[a, 2, r, :], at(dx=w))

    def cross(s):
        i = POS[s]
        for a in range(3):
            for slot in (0, 1, 2) if s in DIRECT else (1,):
                for copy in b1[s, a, slot]:
                    copy.wait_recv()
            if s not in DIRECT:
                b2[s, a].wait_recv()
            for h in (0, 1):
                r = rows(s, (yh if h == 0 else 1 - yh) * HALF, HALF)
                v = pf[a, x, r, :] + rb[a, 1, r, :].astype(F32) + rb[a, 2, r, :].astype(F32)
                if s in DIRECT:
                    v = v + rb[a, 0, r, :].astype(F32)
                if h == 0:
                    own[i, a] = v
                else:
                    sy[i, a] = v
        by[s] = send(sy.at[i], ry.at[i], at(dyh=1))

    def finish(s):
        i = POS[s]
        by[s].wait_recv()
        gate = own[i, 0] + ry[i, 0]
        up = own[i, 1] + ry[i, 1]
        back = own[i, 2] + ry[i, 2]
        sigma = 1.0 / (1.0 + jnp.exp(-gate))
        silu = gate * sigma
        r = rows(s, yh * HALF, HALF)
        hid[2, x, r, :] = (back * silu).astype(BF)
        hid[0, x, r, :] = (silu * up).astype(BF)
        hid[1, x, r, :] = (back * up * sigma * (1.0 + gate * (1.0 - sigma))).astype(BF)
        for a in PATHS[s]:
            w = ways(s)[a]
            src = hid.at[a, x, r, :]
            cx[s, a, 0] = send(src, src, at(dx=w))
            cx[s, a, 1] = send(src, src, at(dx=-w))
            if s in DIRECT:
                cr[s, a] = send(src, src, at(dx=2))
        n = 3 - len(PATHS[s])
        if n:
            src = hid.at[pl.ds(0, n), x, r, :]
            cy[s] = send(src, src, at(dyh=1))

    def spreadA(s, a):
        w = ways(s)[a]
        cx[s, a, 0].wait_recv()
        src = hid.at[a, xi(-w), rows(s, yh * HALF, HALF), :]
        cr[s, a] = send(src, src, at(dx=w))

    def spreadB(s):
        r = rows(s, 0, PLANE)
        cy[s].wait_recv()
        for a in range(3 - len(PATHS[s])):
            w = ways(s)[a]
            src = hid.at[a, x, r, :]
            cx[s, a, 0] = send(src, src, at(dx=w))
            cx[s, a, 1] = send(src, src, at(dx=-w))
            if s in DIRECT:
                cr[s, a] = send(src, src, at(dx=2))

    def onward(s, a):
        w = ways(s)[a]
        cx[s, a, 0].wait_recv()
        src = hid.at[a, xi(-w), rows(s, 0, PLANE), :]
        cr[s, a] = send(src, src, at(dx=w))

    def onwardY(s):
        for a in PATHS[s]:
            if s in DIRECT:
                cx[s, a, 0].wait_recv()
            cx[s, a, 1].wait_recv()
            cr[s, a].wait_recv()
        n = len(PATHS[s])
        src = hid.at[pl.ds(3 - n, n), pl.ds(0, NX), rows(s, yh * HALF, HALF), :]
        gy[s] = send(src, src, at(dyh=1))

    def wide(a, r):
        return jnp.concatenate([hid[a, j, r, :] for j in range(NX)], axis=1)

    def down(s):
        i = POS[s]
        r = rows(s, 0, PLANE)
        for a in range(3 - len(PATHS[s])):
            if s in DIRECT:
                cx[s, a, 0].wait_recv()
            cx[s, a, 1].wait_recv()
            cr[s, a].wait_recv()
        if PATHS[s]:
            gy[s].wait_recv()
        v = lax.dot_general(wide(1, r), wg[...], LL, preferred_element_type=F32)
        v = v + lax.dot_general(wide(2, r), wu[...], LL, preferred_element_type=F32)
        dpart[i] = v
        dsend[i] = dpart[i, pl.ds(pl.multiple_of((1 - k) * HALF, 8), HALF), :]
        dc[s] = send(dsend.at[i], drecv.at[i], at(dk=1))

    def homeward(s):
        i = POS[s]
        dc[s].wait_recv()
        v = dpart[i, pl.ds(pl.multiple_of(k * HALF, 8), HALF), :] + drecv[i]
        zsend[i] = v.astype(BF)
        dpart[i, 0:HALF, :] = v
        index = (count[0], count[0] + 1)
        count[0] += 2
        over = pltpu.make_async_remote_copy(
            src_ref=zsend.at[i], dst_ref=zrecv.at[i], send_sem=ss.at[index[0]], recv_sem=rs.at[index[0]],
            device_id=at(dyl=1), device_id_type=MESH,
        )
        yh_[s] = over, index[1]

        @pl.when(jnp.logical_not(home))
        def _():
            over.start()

    def depart(s):
        i = POS[s]
        over, index = yh_[s]
        if s:
            go = pltpu.make_async_remote_copy(
                src_ref=zsend.at[i], dst_ref=zhome.at[i], send_sem=ss.at[index], recv_sem=rs.at[index],
                device_id=at(dz=s), device_id_type=MESH,
            )
            dz_[s] = go

        @pl.when(home)
        def _():
            over.wait_recv()
            v = dpart[i, 0:HALF, :] + zrecv[i].astype(F32)
            if s == 0:
                zsum[...] = v
            else:
                zsend[i] = v.astype(BF)
                go.start()

        @pl.when(jnp.logical_not(home))
        def _():
            over.wait_send()

    def weights(first, count, start, last, only=None):
        n = count * PLANE
        r = pl.ds(first * PLANE, n)
        for a, out in enumerate((gwd_h, gwg_h, gwu_h)):
            if only is not None and a != only:
                continue
            for j in range(2):
                pair = jnp.concatenate([hid[a, 2 * j, r, :], hid[a, 2 * j + 1, r, :]], axis=1)
                v = lax.dot_general(pair, tc[1 if a == 0 else 0, r, :], FF, preferred_element_type=F32)
                where = acc.at[a, pl.ds(j * 256, 256), :]
                if not start:
                    v = where[...] + v
                if not last:
                    where[...] = v
                elif a == 0:
                    stage[0, pl.ds(j * 256, 256), :] = v.astype(BF)
                else:
                    (wg if a == 1 else wu)[:, j * 256 : (j + 1) * 256] = v.T.astype(BF)
            if last:
                src = stage.at[0] if a == 0 else (wg if a == 1 else wu)
                store = pltpu.make_async_copy(src, out, ls.at[a])
                store.start()
                stores.append(store)

    near = pltpu.make_async_remote_copy(
        src_ref=fin.at[pl.ds(pl.multiple_of((1 - k) * SHARD, 8), SHARD), :], dst_ref=frecv,
        send_sem=ss.at[NSEM], recv_sem=rs.at[NSEM], device_id=at(dk=1), device_id_type=MESH,
    )

    def fin_send():
        @pl.when(home)
        def _():
            total = zsum[...]
            for s in dz_:
                dz_[s].wait_recv()
                total = total + zhome[POS[s]].astype(F32)
            fin[...] = total
            near.start()

    stores = []
    table = dict(
        start2=start2,
        arrive=arrive, partial=partial, relay=relay, cross=cross, finish=finish, spreadA=spreadA, spreadB=spreadB,
        onward=onward, onwardY=onwardY, down=down, homeward=homeward, depart=depart, weights=weights, fin=fin_send,
    )
    for name, *where in PROGRAM:
        table[name](*where)

    @pl.when(home)
    def _():
        gt_out[...] = fin[pl.ds(pl.multiple_of(k * SHARD, 8), SHARD), :]
        near.wait_send()
        for s in dz_:
            dz_[s].wait_send()

    @pl.when(jnp.logical_not(home))
    def _():
        near.wait_recv()
        gt_out[...] = frecv[...]

    for copy in pending:
        copy.wait_send()
    for store in stores:
        store.wait()


def hand_over(g_in, a_in, b_in, c_in, g_out, a_out, b_out, c_out, g, a, b, c, into, out, g_sem):
    first, second = [], []
    get = pltpu.make_async_copy(g_in, g, g_sem)
    for i, (src, via, dst) in enumerate(((c_in, c, c_out), (a_in, a, a_out), (b_in, b, b_out))):
        n = src.shape[0] // 2
        for j in range(2):
            part = pl.ds(j * n, n)
            first.append(pltpu.make_async_copy(src.at[part, :], via.at[part, :], into.at[i, j]))
            second.append(pltpu.make_async_copy(via.at[part, :], dst.at[part, :], out.at[i, j]))
    get.start()
    for copy in first:
        copy.start()
    for before, after in zip(first, second):
        before.wait()
        after.start()
    get.wait()
    g_out[...] = g[...].astype(BF)
    for copy in second:
        copy.wait()


def local(tokens, cotangent, w_gate, w_up, w_down):
    vm = pl.BlockSpec(memory_space=pltpu.VMEM)
    hbm = pl.BlockSpec(memory_space=pl.ANY)
    V = pltpu.VMEM
    shapes = [jax.ShapeDtypeStruct(s, BF) for s in ((SHARD, WIDE), (WIDE, 512), (WIDE, 512), (512, WIDE))]
    grads = pl.pallas_call(
        kernel,
        out_shape=[jax.ShapeDtypeStruct((SHARD, WIDE), F32)] + shapes[1:],
        in_specs=[vm, vm, hbm, hbm, hbm],
        out_specs=[vm, hbm, hbm, hbm],
        scratch_shapes=[
            V((WIDE, 512), BF), V((WIDE, 512), BF), V((512, WIDE), BF),
            V((2, ROWS, WIDE), BF),
            V((3, NX, ROWS, LANE), F32),
            V((3, NX, ROWS, LANE), BF),
            V((3, 3, ROWS, LANE), BF),
            V((NZ, 3, HALF, LANE), F32),
            V((NZ, 3, HALF, LANE), F32),
            V((NZ, 3, HALF, LANE), F32),
            V((3, NX, ROWS, LANE), BF),
            V((NZ, PLANE, WIDE), F32),
            V((NZ, HALF, WIDE), F32),
            V((NZ, HALF, WIDE), F32),
            V((NZ, HALF, WIDE), BF),
            V((NZ, HALF, WIDE), BF),
            V((NZ, HALF, WIDE), BF),
            V((HALF, WIDE), F32),
            V((3, 512, WIDE), F32),
            V((1, 512, WIDE), BF),
            V((SHARD, WIDE), F32), V((SHARD, WIDE), F32),
            V((HALF, WIDE), F32), V((SHARD, WIDE), F32),
            pltpu.SemaphoreType.DMA((NSEM + 1,)),
            pltpu.SemaphoreType.DMA((NSEM + 1,)),
            pltpu.SemaphoreType.DMA((3,)),
        ],
        compiler_params=pltpu.CompilerParams(
            collective_id=0, has_side_effects=True, vmem_limit_bytes=62 * 2**20
        ),
        name="ffn_backward",
    )(tokens, cotangent, w_gate, w_up, w_down)
    return pl.pallas_call(
        hand_over,
        out_shape=shapes,
        in_specs=[hbm] * 4,
        out_specs=[vm, hbm, hbm, hbm],
        scratch_shapes=[V((SHARD, WIDE), F32)]
        + [V(s.shape, BF) for s in shapes[1:]]
        + [pltpu.SemaphoreType.DMA((3, 2))] * 2
        + [pltpu.SemaphoreType.DMA],
        name="hand_over",
    )(*grads)


def solution(mesh):
    return jax.shard_map(
        local,
        mesh=mesh,
        in_specs=(P("col", "row"), P("col", "row"), P("row", "col"), P("row", "col"), P("col", "row")),
        out_specs=(P("col", "row"), P("row", "col"), P("row", "col"), P("col", "row")),
        check_vma=False,
    )
```

```python
import jax
import jax.numpy as jnp
from jax import lax
from jax.experimental import pallas as pl
from jax.experimental.pallas import tpu as pltpu
from jax.sharding import PartitionSpec as P

MESH = pl.DeviceIdType.MESH
BF = jnp.bfloat16
F32 = jnp.float32
LL = (((1,), (1,)), ((), ()))
FF = (((0,), (0,)), ((), ()))

SHARD = 40
HALF = 80
PLANE = 160
NZ = 8
NX = 4
ROWS = NZ * PLANE
WIDE = 896
LANE = 128
NSEM = 280
DOWN = (1, 7, 2, 6, 3, 5, 4, 0)
POS = {s: i for i, s in enumerate(DOWN)}
PATHS = {0: (), 1: (2,), 2: (2,), 3: (2,), 4: (2,), 5: (2,), 6: (2,), 7: (2,)}
DIRECT = ()
PROGRAM = (
    ('partial', 0, 0),
    ('start2',),
    ('arrive', 7, 0),
    ('arrive', 1, 0),
    ('partial', 0, 1),
    ('arrive', 7, 1),
    ('relay', 0, 2),
    ('arrive', 1, 1),
    ('relay', 0, 0),
    ('partial', 7),
    ('arrive', 6, 0),
    ('partial', 1),
    ('arrive', 6, 1),
    ('arrive', 2, 0),
    ('relay', 0, 1),
    ('partial', 6),
    ('relay', 7, 2),
    ('arrive', 5, 0),
    ('arrive', 2, 1),
    ('relay', 1, 0),
    ('relay', 7, 0),
    ('relay', 1, 1),
    ('relay', 1, 2),
    ('arrive', 5, 1),
    ('arrive', 3, 0),
    ('relay', 6, 0),
    ('cross', 0),
    ('relay', 6, 1),
    ('relay', 7, 1),
    ('partial', 5),
    ('arrive', 3, 1),
    ('cross', 1),
    ('relay', 6, 2),
    ('partial', 3),
    ('cross', 7),
    ('relay', 5, 0),
    ('arrive', 4, 0),
    ('arrive', 4, 1),
    ('relay', 5, 1),
    ('relay', 5, 2),
    ('cross', 6),
    ('partial', 4),
    ('relay', 3, 1),
    ('relay', 3, 2),
    ('relay', 3, 0),
    ('finish', 0),
    ('partial', 2),
    ('finish', 1),
    ('cross', 5),
    ('relay', 4, 2),
    ('relay', 4, 1),
    ('relay', 4, 0),
    ('finish', 6),
    ('cross', 3),
    ('finish', 7),
    ('relay', 2, 0),
    ('relay', 2, 1),
    ('spreadA', 1, 2),
    ('relay', 2, 2),
    ('spreadB', 1),
    ('finish', 5),
    ('cross', 4),
    ('spreadA', 7, 2),
    ('spreadB', 6),
    ('finish', 3),
    ('spreadB', 7),
    ('cross', 2),
    ('spreadA', 6, 2),
    ('onwardY', 7),
    ('spreadB', 5),
    ('spreadA', 3, 2),
    ('spreadA', 5, 2),
    ('onward', 1, 1),
    ('onward', 1, 0),
    ('finish', 4),
    ('onwardY', 6),
    ('spreadB', 3),
    ('finish', 2),
    ('onwardY', 5),
    ('onward', 5, 0),
    ('onward', 5, 1),
    ('onward', 6, 0),
    ('spreadA', 4, 2),
    ('onward', 3, 0),
    ('onwardY', 3),
    ('spreadB', 4),
    ('spreadA', 2, 2),
    ('onward', 3, 1),
    ('onwardY', 1),
    ('onwardY', 4),
    ('spreadB', 2),
    ('onward', 7, 1),
    ('down', 5),
    ('onward', 4, 0),
    ('onward', 4, 1),
    ('onwardY', 2),
    ('onward', 6, 1),
    ('onward', 7, 0),
    ('spreadB', 0),
    ('down', 3),
    ('homeward', 5),
    ('down', 1),
    ('homeward', 3),
    ('onward', 2, 1),
    ('onward', 2, 0),
    ('down', 4),
    ('homeward', 1),
    ('down', 7),
    ('depart', 5),
    ('down', 6),
    ('homeward', 4),
    ('depart', 3),
    ('onward', 0, 2),
    ('down', 2),
    ('homeward', 6),
    ('homeward', 2),
    ('depart', 4),
    ('onward', 0, 0),
    ('onward', 0, 1),
    ('weights', 0, 4, True, False, 0),
    ('homeward', 7),
    ('depart', 6),
    ('weights', 0, 4, True, False, 1),
    ('depart', 2),
    ('down', 0),
    ('depart', 7),
    ('weights', 0, 4, True, False, 2),
    ('weights', 4, 4, False, True, 0),
    ('homeward', 0),
    ('depart', 1),
    ('weights', 4, 4, False, True, 1),
    ('weights', 4, 4, False, True, 2),
    ('depart', 0),
)


def kernel(
    tok, cot, wg_h, wu_h, wd_h,
    gt_out, gwg_h, gwu_h, gwd_h,
    wg, wu, wd, tc, pf, pb, rb, sy, ry, own, hid,
    dpart, dsend, drecv, zsend, zrecv, zhome, zsum, acc, stage, xs, xr, fin, frecv,
    ss, rs, ls,
):
    row, col = lax.axis_index("row"), lax.axis_index("col")
    yh, x = row // NX, row % NX
    z, yl, k = col // 4, (col // 2) % 2, col % 2

    def at(dyh=0, dx=0, dz=0, dyl=0, dk=0):
        r = ((yh + dyh) % 2) * NX + (x + dx + NX) % NX
        c = ((z + dz + NZ) % NZ) * 4 + ((yl + dyl) % 2) * 2 + (k + dk) % 2
        return (r, c)

    def xi(d):
        return (x + d + NX) % NX

    count = [0]
    pending = []

    def send(src, dst, to, hold=True):
        i = count[0]
        count[0] += 1
        copy = pltpu.make_async_remote_copy(
            src_ref=src, dst_ref=dst, send_sem=ss.at[i], recv_sem=rs.at[i], device_id=to, device_id_type=MESH
        )
        copy.start()
        if hold:
            pending.append(copy)
        return copy

    loads = []
    for i, (src, dst) in enumerate(((wg_h, wg), (wu_h, wu), (wd_h, wd))):
        load = pltpu.make_async_copy(src, dst, ls.at[i])
        load.start()
        loads.append(load)

    partners = [at(dx=1), at(dx=-1), at(dx=2), at(dyh=1), at(dk=1), at(dyl=1)]
    partners += [at(dz=d) for d in range(1, NZ)]
    barrier = pltpu.get_barrier_semaphore()
    for p in partners:
        pl.semaphore_signal(barrier, inc=1, device_id=p, device_id_type=MESH)
    mine = jnp.where(k == 0, tok[...].astype(F32), cot[...].astype(F32))
    xs[...] = jnp.where(k == 0, cot[...].astype(F32), tok[...].astype(F32))
    pl.semaphore_wait(barrier, len(partners))

    def rows(s, start, size):
        return pl.ds(pl.multiple_of(POS[s] * PLANE + start, 16), size)

    first = send(xs, xr, at(dk=1))
    first.wait_recv()
    other = xr[...]
    low = jnp.where(k == 0, mine, other)
    high = jnp.where(k == 0, other, mine)
    both = jnp.concatenate([low, high], axis=0).astype(BF)
    tc[k, rows(0, yl * HALF, HALF), :] = both

    halves = (yl * HALF, (1 - yl) * HALF)
    ring = {}
    twin = {}

    def to_twin(s, h):
        ref = tc.at[k, rows(s, halves[h], HALF), :]
        twin[s, h] = send(ref, ref, at(dk=1))

    def to_ring(s, h, step):
        t = (s - step) % NZ
        src = tc.at[k, rows(s, halves[h], HALF), :]
        ring[t, h] = send(src, tc.at[k, rows(t, halves[h], HALF), :], at(dz=step))

    ref0 = tc.at[k, rows(0, halves[0], HALF), :]
    across = send(ref0, ref0, at(dyl=1))
    to_twin(0, 0)
    to_ring(0, 0, -1)
    to_ring(0, 0, 1)
    def start2():
        across.wait_recv()
        to_twin(0, 1)
        to_ring(0, 1, -1)
        to_ring(0, 1, 1)

    for load in loads:
        load.wait()

    def arrive(s, h):
        ring[s, h].wait_recv()
        to_twin(s, h)
        if s in (1, 2) or (s == 3 and h == 0):
            to_ring(s, h, -1)
        if s in (7, 6) or (s == 5 and h == 1):
            to_ring(s, h, 1)

    def ways(s):
        return (1, -1, 1 if POS[s] % 2 == 0 else -1)

    b1, b2, by, cy, cx, cr, gy, dc, yh_, dz_ = {}, {}, {}, {}, {}, {}, {}, {}, {}, {}
    home = yl == k

    def partial(s, half=None):
        for h in (0, 1) if half is None else (half,):
            twin[s, h].wait_recv()
        r = rows(s, 0, PLANE) if half is None else rows(s, halves[half], HALF)
        t = tc[0, r, :]
        c = tc[1, r, :]
        for a in range(3):
            if a == 0:
                v = jnp.dot(t, wg[...], preferred_element_type=F32)
            elif a == 1:
                v = jnp.dot(t, wu[...], preferred_element_type=F32)
            else:
                v = lax.dot_general(c, wd[...], LL, preferred_element_type=F32)
            for j in range(NX):
                piece = v[:, j * LANE : (j + 1) * LANE]
                pf[a, j, r, :] = piece
                pb[a, j, r, :] = piece.astype(BF)
            w = ways(s)[a]
            if s in DIRECT:
                plan = ((0, w, w), (1, -w, -w), (2, 2, 2))
            else:
                plan = ((0, 2, w), (1, -w, -w))
            for slot, block, to in plan:
                copy = send(pb.at[a, xi(block), r, :], rb.at[a, slot, r, :], at(dx=to))
                b1.setdefault((s, a, slot), []).append(copy)

    def relay(s, a):
        r = rows(s, 0, PLANE)
        w = ways(s)[a]
        for copy in b1[s, a, 0]:
            copy.wait_recv()
        pb[a, xi(w), r, :] = (pf[a, xi(w), r, :] + rb[a, 0, r, :].astype(F32)).astype(BF)
        b2[s, a] = send(pb.at[a, xi(w), r, :], rb.at[a, 2, r, :], at(dx=w))

    def cross(s):
        i = POS[s]
        for a in range(3):
            for slot in (0, 1, 2) if s in DIRECT else (1,):
                for copy in b1[s, a, slot]:
                    copy.wait_recv()
            if s not in DIRECT:
                b2[s, a].wait_recv()
            for h in (0, 1):
                r = rows(s, (yh if h == 0 else 1 - yh) * HALF, HALF)
                v = pf[a, x, r, :] + rb[a, 1, r, :].astype(F32) + rb[a, 2, r, :].astype(F32)
                if s in DIRECT:
                    v = v + rb[a, 0, r, :].astype(F32)
                if h == 0:
                    own[i, a] = v
                else:
                    sy[i, a] = v
        by[s] = send(sy.at[i], ry.at[i], at(dyh=1))

    def finish(s):
        i = POS[s]
        by[s].wait_recv()
        gate = own[i, 0] + ry[i, 0]
        up = own[i, 1] + ry[i, 1]
        back = own[i, 2] + ry[i, 2]
        sigma = 1.0 / (1.0 + jnp.exp(-gate))
        silu = gate * sigma
        r = rows(s, yh * HALF, HALF)
        hid[2, x, r, :] = (back * silu).astype(BF)
        hid[0, x, r, :] = (silu * up).astype(BF)
        hid[1, x, r, :] = (back * up * sigma * (1.0 + gate * (1.0 - sigma))).astype(BF)
        for a in PATHS[s]:
            w = ways(s)[a]
            src = hid.at[a, x, r, :]
            cx[s, a, 0] = send(src, src, at(dx=w))
            cx[s, a, 1] = send(src, src, at(dx=-w))
            if s in DIRECT:
                cr[s, a] = send(src, src, at(dx=2))
        n = 3 - len(PATHS[s])
        if n:
            src = hid.at[pl.ds(0, n), x, r, :]
            cy[s] = send(src, src, at(dyh=1))

    def spreadA(s, a):
        w = ways(s)[a]
        cx[s, a, 0].wait_recv()
        src = hid.at[a, xi(-w), rows(s, yh * HALF, HALF), :]
        cr[s, a] = send(src, src, at(dx=w))

    def spreadB(s):
        r = rows(s, 0, PLANE)
        cy[s].wait_recv()
        for a in range(3 - len(PATHS[s])):
            w = ways(s)[a]
            src = hid.at[a, x, r, :]
            cx[s, a, 0] = send(src, src, at(dx=w))
            cx[s, a, 1] = send(src, src, at(dx=-w))
            if s in DIRECT:
                cr[s, a] = send(src, src, at(dx=2))

    def onward(s, a):
        w = ways(s)[a]
        cx[s, a, 0].wait_recv()
        src = hid.at[a, xi(-w), rows(s, 0, PLANE), :]
        cr[s, a] = send(src, src, at(dx=w))

    def onwardY(s):
        for a in PATHS[s]:
            if s in DIRECT:
                cx[s, a, 0].wait_recv()
            cx[s, a, 1].wait_recv()
            cr[s, a].wait_recv()
        n = len(PATHS[s])
        src = hid.at[pl.ds(3 - n, n), pl.ds(0, NX), rows(s, yh * HALF, HALF), :]
        gy[s] = send(src, src, at(dyh=1))

    def wide(a, r):
        return jnp.concatenate([hid[a, j, r, :] for j in range(NX)], axis=1)

    def down(s):
        i = POS[s]
        r = rows(s, 0, PLANE)
        for a in range(3 - len(PATHS[s])):
            if s in DIRECT:
                cx[s, a, 0].wait_recv()
            cx[s, a, 1].wait_recv()
            cr[s, a].wait_recv()
        if PATHS[s]:
            gy[s].wait_recv()
        if s == 0:
            for h in (1 - k, k):
                half = rows(s, h * HALF, HALF)
                v = lax.dot_general(wide(1, half), wg[...], LL, preferred_element_type=F32)
                v = v + lax.dot_general(wide(2, half), wu[...], LL, preferred_element_type=F32)
                if s in dc:
                    dpart[i, pl.ds(pl.multiple_of(k * HALF, 8), HALF), :] = v
                else:
                    dsend[i] = v
                    dc[s] = send(dsend.at[i], drecv.at[i], at(dk=1))
            return
        v = lax.dot_general(wide(1, r), wg[...], LL, preferred_element_type=F32)
        v = v + lax.dot_general(wide(2, r), wu[...], LL, preferred_element_type=F32)
        dpart[i] = v
        dsend[i] = dpart[i, pl.ds(pl.multiple_of((1 - k) * HALF, 8), HALF), :]
        dc[s] = send(dsend.at[i], drecv.at[i], at(dk=1))

    def homeward(s):
        i = POS[s]
        dc[s].wait_recv()
        v = dpart[i, pl.ds(pl.multiple_of(k * HALF, 8), HALF), :] + drecv[i]
        zsend[i] = v.astype(BF)
        dpart[i, 0:HALF, :] = v
        index = (count[0], count[0] + 1)
        count[0] += 2
        over = pltpu.make_async_remote_copy(
            src_ref=zsend.at[i], dst_ref=zrecv.at[i], send_sem=ss.at[index[0]], recv_sem=rs.at[index[0]],
            device_id=at(dyl=1), device_id_type=MESH,
        )
        yh_[s] = over, index[1]

        @pl.when(jnp.logical_not(home))
        def _():
            over.start()

    def depart(s):
        i = POS[s]
        over, index = yh_[s]
        if s:
            go = pltpu.make_async_remote_copy(
                src_ref=zsend.at[i], dst_ref=zhome.at[i], send_sem=ss.at[index], recv_sem=rs.at[index],
                device_id=at(dz=s), device_id_type=MESH,
            )
            dz_[s] = go

        @pl.when(home)
        def _():
            if s == 0:
                total = dpart[i, 0:HALF, :]
                for d in dz_:
                    dz_[d].wait_recv()
                    total = total + zhome[POS[d]].astype(F32)
                zsum[...] = total
            over.wait_recv()
            if s == 0:
                fin[...] = zsum[...] + zrecv[i].astype(F32)
                near.start()
            else:
                v = dpart[i, 0:HALF, :] + zrecv[i].astype(F32)
                zsend[i] = v.astype(BF)
                go.start()

        @pl.when(jnp.logical_not(home))
        def _():
            over.wait_send()

    def weights(first, count, start, last, only=None):
        n = count * PLANE
        r = pl.ds(first * PLANE, n)
        for a, out in enumerate((gwd_h, gwg_h, gwu_h)):
            if only is not None and a != only:
                continue
            for j in range(2):
                pair = jnp.concatenate([hid[a, 2 * j, r, :], hid[a, 2 * j + 1, r, :]], axis=1)
                v = lax.dot_general(pair, tc[1 if a == 0 else 0, r, :], FF, preferred_element_type=F32)
                where = acc.at[a, pl.ds(j * 256, 256), :]
                if not start:
                    v = where[...] + v
                if not last:
                    where[...] = v
                elif a == 0:
                    stage[0, pl.ds(j * 256, 256), :] = v.astype(BF)
                else:
                    (wg if a == 1 else wu)[:, j * 256 : (j + 1) * 256] = v.T.astype(BF)
            if last:
                src = stage.at[0] if a == 0 else (wg if a == 1 else wu)
                store = pltpu.make_async_copy(src, out, ls.at[a])
                store.start()
                stores.append(store)

    near = pltpu.make_async_remote_copy(
        src_ref=fin.at[pl.ds(pl.multiple_of((1 - k) * SHARD, 8), SHARD), :], dst_ref=frecv,
        send_sem=ss.at[NSEM], recv_sem=rs.at[NSEM], device_id=at(dk=1), device_id_type=MESH,
    )

    stores = []
    table = dict(
        start2=start2,
        arrive=arrive, partial=partial, relay=relay, cross=cross, finish=finish, spreadA=spreadA, spreadB=spreadB,
        onward=onward, onwardY=onwardY, down=down, homeward=homeward, depart=depart, weights=weights,
    )
    for name, *where in PROGRAM:
        table[name](*where)

    @pl.when(home)
    def _():
        gt_out[...] = fin[pl.ds(pl.multiple_of(k * SHARD, 8), SHARD), :]
        near.wait_send()
        for s in dz_:
            dz_[s].wait_send()

    @pl.when(jnp.logical_not(home))
    def _():
        near.wait_recv()
        gt_out[...] = frecv[...]

    for copy in pending:
        copy.wait_send()
    for store in stores:
        store.wait()


def hand_over(g_in, a_in, b_in, c_in, g_out, a_out, b_out, c_out, g, a, b, c, into, out, g_sem):
    first, second = [], []
    get = pltpu.make_async_copy(g_in, g, g_sem)
    for i, (src, via, dst) in enumerate(((c_in, c, c_out), (a_in, a, a_out), (b_in, b, b_out))):
        n = src.shape[0] // 2
        for j in range(2):
            part = pl.ds(j * n, n)
            first.append(pltpu.make_async_copy(src.at[part, :], via.at[part, :], into.at[i, j]))
            second.append(pltpu.make_async_copy(via.at[part, :], dst.at[part, :], out.at[i, j]))
    get.start()
    for copy in first:
        copy.start()
    for before, after in zip(first, second):
        before.wait()
        after.start()
    get.wait()
    g_out[...] = g[...].astype(BF)
    for copy in second:
        copy.wait()


def local(tokens, cotangent, w_gate, w_up, w_down):
    vm = pl.BlockSpec(memory_space=pltpu.VMEM)
    hbm = pl.BlockSpec(memory_space=pl.ANY)
    V = pltpu.VMEM
    shapes = [jax.ShapeDtypeStruct(s, BF) for s in ((SHARD, WIDE), (WIDE, 512), (WIDE, 512), (512, WIDE))]
    grads = pl.pallas_call(
        kernel,
        out_shape=[jax.ShapeDtypeStruct((SHARD, WIDE), F32)] + shapes[1:],
        in_specs=[vm, vm, hbm, hbm, hbm],
        out_specs=[vm, hbm, hbm, hbm],
        scratch_shapes=[
            V((WIDE, 512), BF), V((WIDE, 512), BF), V((512, WIDE), BF),
            V((2, ROWS, WIDE), BF),
            V((3, NX, ROWS, LANE), F32),
            V((3, NX, ROWS, LANE), BF),
            V((3, 3, ROWS, LANE), BF),
            V((NZ, 3, HALF, LANE), F32),
            V((NZ, 3, HALF, LANE), F32),
            V((NZ, 3, HALF, LANE), F32),
            V((3, NX, ROWS, LANE), BF),
            V((NZ, PLANE, WIDE), F32),
            V((NZ, HALF, WIDE), F32),
            V((NZ, HALF, WIDE), F32),
            V((NZ, HALF, WIDE), BF),
            V((NZ, HALF, WIDE), BF),
            V((NZ, HALF, WIDE), BF),
            V((HALF, WIDE), F32),
            V((3, 512, WIDE), F32),
            V((1, 512, WIDE), BF),
            V((SHARD, WIDE), F32), V((SHARD, WIDE), F32),
            V((HALF, WIDE), F32), V((SHARD, WIDE), F32),
            pltpu.SemaphoreType.DMA((NSEM + 1,)),
            pltpu.SemaphoreType.DMA((NSEM + 1,)),
            pltpu.SemaphoreType.DMA((3,)),
        ],
        compiler_params=pltpu.CompilerParams(
            collective_id=0, has_side_effects=True, vmem_limit_bytes=62 * 2**20
        ),
        name="ffn_backward",
    )(tokens, cotangent, w_gate, w_up, w_down)
    return pl.pallas_call(
        hand_over,
        out_shape=shapes,
        in_specs=[hbm] * 4,
        out_specs=[vm, hbm, hbm, hbm],
        scratch_shapes=[V((SHARD, WIDE), F32)]
        + [V(s.shape, BF) for s in shapes[1:]]
        + [pltpu.SemaphoreType.DMA((3, 2))] * 2
        + [pltpu.SemaphoreType.DMA],
        name="hand_over",
    )(*grads)


def solution(mesh):
    return jax.shard_map(
        local,
        mesh=mesh,
        in_specs=(P("col", "row"), P("col", "row"), P("row", "col"), P("row", "col"), P("col", "row")),
        out_specs=(P("col", "row"), P("row", "col"), P("row", "col"), P("col", "row")),
        check_vma=False,
    )
```
